32 devices in a mesh: dp: 2 (over x), depth: 2 (over y), tensor: 8 (over z, core).
Axes of the slice: x: 2, y: 2, z: 4, core: 2. Of those that a mesh axis runs over, the one named last changes fastest.
Arguments:
- text: bfloat16 [256, 8192], P(('dp', 'tensor')), may hold values from -6 to 6
- vision: bfloat16 [512, 8192], P(('dp', 'depth'), 'tensor'), may hold values from -6 to 6
- query_weight: bfloat16 [2, 8192, 2048], P('depth', None, 'tensor'), may hold values from -0.0625 to 0.0625
- key_weight: bfloat16 [2, 8192, 256], P('depth', 'tensor'), may hold values from -0.0625 to 0.0625
- value_weight: bfloat16 [2, 8192, 256], P('depth', 'tensor'), may hold values from -0.0625 to 0.0625
- out_weight: bfloat16 [2, 2048, 8192], P('depth', 'tensor'), may hold values from -0.25 to 0.25
- gate: float32 [2], P('depth'), may hold values from 0.5 to 1.5
- cotangent: bfloat16 [256, 8192], P(('dp', 'tensor')), may hold values from -0.75 to 0.75
- tile_table: int32 [2, 8, 4], P('dp'), may hold values 0 or 1
- vision_tiles: int32 [2], P('dp'), may hold values from 1 to 4
- text_lengths: int32 [2], P('dp'), may hold values from 64 to 128
Outputs:
- hidden_states: bfloat16 [2, 256, 8192], P('depth', ('dp', 'tensor'))
- text_grads: bfloat16 [2, 256, 8192], P('depth', ('dp', 'tensor'))
- vision_grad: float32 [512, 8192], P(('dp', 'depth'), 'tensor')
- key_weight_grad: float32 [2, 8192, 256], P('depth', 'tensor', 'dp')
- value_weight_grad: float32 [2, 8192, 256], P('depth', 'tensor', 'dp')
The draws below stay inside these ranges and needn't reach their ends.
All inputs are finite; a program needn't handle non-finite values. No bound on the sum of `tile_table` on one device may be relied on, other than what follows from the above.
Results may differ from the reference program's by a relative error of at most 0.034.
Values may be sent and summed in bfloat16 or wider, within the bound.
A program may use at most 128 MiB of HBM per device.

```python
import math
import jax
import jax.numpy as jnp
from jax import lax

D = 8192
HD = 128
HEAD_DEV = 2
QGROUP = 8
SEQ = 128
TBLK = 16
TILES = 4
TILE_ROWS = 64
LAYERS = 2
HEADS = 16
KVH = 2
VIS = 256
N_DP = 2
N_TENSOR = 8


def plant(values, rng, smallest, top_value):
    shape = values.shape
    place = [jax.random.randint(jax.random.fold_in(rng, axis), (), 0, shape[axis]) for axis in range(len(shape))]
    values = values.at[tuple(place)].set(smallest)
    longest = shape.index(max(shape))
    place[longest] = (place[longest] + 1) % shape[longest]
    return values.at[tuple(place)].set(top_value)


def level_of(stream_key, extent, cuts, least, largest):
    def one(axis_at, parts):
        steps = jax.random.uniform(jax.random.fold_in(jax.random.fold_in(stream_key, 6), axis_at), (parts,), jnp.float32, least / len(cuts), largest / len(cuts))
        return jnp.repeat(jnp.exp(steps), extent[axis_at] // parts).reshape((-1,) + (1,) * (len(extent) - axis_at - 1))

    gain = one(*cuts[0])
    for cut in cuts[1:]:
        gain = gain * one(*cut)
    return gain


def gaussian(key, shape, deviation, limit, pieces=(), held_as=jnp.bfloat16):
    loudness = level_of(key, shape, pieces, -0.22, 0.18) if pieces else 1.0
    result = jax.random.normal(key, shape, jnp.float32) * deviation * loudness
    return jnp.minimum(jnp.maximum(result, -limit), limit).astype(held_as)


def setup_inputs(seed: int = 0) -> dict:
    splits = jax.random.split(jax.random.key(seed), 12)
    text = gaussian(splits[0], (N_DP * SEQ, D), 1.0, 6.0, ((0, 16),))
    vision = gaussian(splits[1], (N_DP * VIS, D), 1.0, 6.0, ((0, 4), (1, 8)))
    query_weight = gaussian(splits[2], (LAYERS, D, HEADS * HD), D ** -0.5, 0.0625, ((0, 2), (2, 8)))
    key_weight = gaussian(splits[3], (LAYERS, D, KVH * HD), D ** -0.5, 0.0625, ((0, 2), (1, 8)))
    value_weight = gaussian(splits[4], (LAYERS, D, KVH * HD), D ** -0.5, 0.0625, ((0, 2), (1, 8)))
    out_weight = gaussian(splits[5], (LAYERS, HEADS * HD, D), (4 * HD) ** -0.5, 0.25, ((0, 2), (1, 8)))
    gate = jnp.clip(0.5 + 1.0 * jax.random.uniform(splits[6], (LAYERS,), jnp.float32) ** level_of(splits[6], (LAYERS,), ((0, 2),), -0.2, 0.2), 0.5, 1.5)
    cotangent = gaussian(splits[7], (N_DP * SEQ, D), 0.125, 0.75, ((0, 16),))
    tile_table = plant((jax.random.randint(splits[8], (N_DP, SEQ // TBLK, TILES), 0, 3) < 2).astype(jnp.int32), jax.random.fold_in(splits[8], 1), 0, 1)
    vision_tiles = jax.random.randint(splits[9], (N_DP,), 1, TILES + 1).astype(jnp.int32)
    text_lengths = jax.random.randint(splits[10], (N_DP,), SEQ // 2, SEQ + 1).astype(jnp.int32)
    return dict(text=text, vision=vision, query_weight=query_weight, key_weight=key_weight, value_weight=value_weight, out_weight=out_weight, gate=gate, cotangent=cotangent, tile_table=tile_table, vision_tiles=vision_tiles, text_lengths=text_lengths)


def normalize(values, epsilon):
    return values * lax.rsqrt(lax.optimization_barrier(jnp.mean(values * values, axis=-1, keepdims=True)) + epsilon)

def norm_back(values, upstream, epsilon):
    inv_rms = lax.rsqrt(lax.optimization_barrier(jnp.mean(values * values, axis=-1, keepdims=True)) + epsilon)
    normed = values * inv_rms
    return inv_rms * (upstream - normed * lax.optimization_barrier(jnp.mean(upstream * normed, axis=-1, keepdims=True)))

def allowed_mask(table, tile_count, text_count):
    tile_ok = jnp.arange(TILES, dtype=jnp.int32) < tile_count
    block_ok = (table > 0) & tile_ok[None, :]
    full_mask = jnp.broadcast_to(block_ok[:, None, :, None], (SEQ // TBLK, TBLK, TILES, TILE_ROWS)).reshape(SEQ, VIS)
    row_ok = jnp.arange(SEQ, dtype=jnp.int32) < text_count
    return full_mask & row_ok[:, None]

def reference(text, vision, query_weight, key_weight, value_weight, out_weight, gate, cotangent, tile_table, vision_tiles, text_lengths):
    groups = N_TENSOR
    local_width = HEAD_DEV * HD
    inv_sqrt = 1.0 / math.sqrt(HD)
    hidden_all = [[] for layer_at in range(LAYERS)]
    grads_all = [[] for layer_at in range(LAYERS)]
    vision_all = []
    dkey_total = jnp.zeros((LAYERS, D, KVH * HD), jnp.float32)
    dvalue_total = jnp.zeros((LAYERS, D, KVH * HD), jnp.float32)
    for sample in range(N_DP):
        inputs = text[sample * SEQ:(sample + 1) * SEQ]
        vis_rows = vision[sample * VIS:(sample + 1) * VIS]
        allowed = allowed_mask(tile_table[sample], vision_tiles[sample], text_lengths[sample])
        row_live = jnp.any(allowed, axis=-1).astype(jnp.float32)
        kept_all = []
        for layer_at in range(LAYERS):
            key_pre = jnp.dot(vis_rows, key_weight[layer_at], preferred_element_type=jnp.float32).reshape(VIS, KVH, HD)
            key_cast = normalize(key_pre, 1e-06).astype(jnp.bfloat16)
            value_cast = jnp.dot(vis_rows, value_weight[layer_at], preferred_element_type=jnp.float32).astype(jnp.bfloat16).reshape(VIS, KVH, HD)
            inputs_f = inputs.astype(jnp.float32)
            normed = normalize(inputs_f, 1e-05).astype(jnp.bfloat16)
            query = jnp.dot(normed, query_weight[layer_at], preferred_element_type=jnp.float32).reshape(SEQ, KVH, QGROUP, HD)
            query_cast = normalize(query, 1e-06).astype(jnp.bfloat16)
            scores = jnp.einsum('sgqd,vgd->gqsv', query_cast.astype(jnp.float32), key_cast.astype(jnp.float32)) * inv_sqrt
            expd = jnp.where(allowed, jnp.exp(scores), 0.0)
            probs = expd / (lax.optimization_barrier(jnp.sum(expd, axis=-1, keepdims=True)) + (1.0 - row_live)[:, None])
            probs_cast = probs.astype(jnp.bfloat16)
            mixed = jnp.einsum('gqsv,vgd->sgqd', probs_cast.astype(jnp.float32), value_cast.astype(jnp.float32)).astype(jnp.bfloat16)
            mixed_groups = mixed.reshape(SEQ, groups, local_width).astype(jnp.float32)
            out_groups = out_weight[layer_at].reshape(groups, local_width, D).astype(jnp.float32)
            terms = jnp.einsum('sgk,gkd->gsd', mixed_groups, out_groups).astype(jnp.bfloat16)
            attended = lax.optimization_barrier(jnp.sum(terms.astype(jnp.float32), axis=0))
            gate_value = jnp.tanh(gate[layer_at])
            outputs = (inputs_f + gate_value * attended).astype(jnp.bfloat16)
            kept_all.append((inputs, key_pre, key_cast, value_cast, query, query_cast, probs, probs_cast))
            hidden_all[layer_at].append(outputs)
            inputs = outputs
        upstream = cotangent[sample * SEQ:(sample + 1) * SEQ]
        vision_grad = jnp.zeros((VIS, D), jnp.float32)
        for layer_at in reversed(range(LAYERS)):
            inputs, key_pre, key_cast, value_cast, query, query_cast, probs, probs_cast = kept_all[layer_at]
            gate_value = jnp.tanh(gate[layer_at])
            scaled = (gate_value * upstream.astype(jnp.float32)).astype(jnp.bfloat16)
            dmixed = jnp.dot(scaled, out_weight[layer_at].T, preferred_element_type=jnp.float32).astype(jnp.bfloat16).reshape(SEQ, KVH, QGROUP, HD)
            dprobs = jnp.einsum('sgqd,vgd->gqsv', dmixed.astype(jnp.float32), value_cast.astype(jnp.float32))
            dvalue = jnp.einsum('gqsv,sgqd->vgd', probs_cast.astype(jnp.float32), dmixed.astype(jnp.float32))
            dscores = (probs * (dprobs - lax.optimization_barrier(jnp.sum(probs * dprobs, axis=-1, keepdims=True))) * inv_sqrt).astype(jnp.bfloat16)
            dquery_hat = jnp.einsum('gqsv,vgd->sgqd', dscores.astype(jnp.float32), key_cast.astype(jnp.float32))
            dkey_hat = jnp.einsum('gqsv,sgqd->vgd', dscores.astype(jnp.float32), query_cast.astype(jnp.float32))
            dquery = norm_back(query, dquery_hat, 1e-06).astype(jnp.bfloat16).reshape(SEQ, groups, local_width)
            query_groups = query_weight[layer_at].reshape(D, groups, local_width).astype(jnp.float32)
            terms = jnp.einsum('sgk,dgk->gsd', dquery.astype(jnp.float32), query_groups).astype(jnp.bfloat16)
            dnormed = lax.optimization_barrier(jnp.sum(terms.astype(jnp.float32), axis=0))
            dinputs = (upstream.astype(jnp.float32) + norm_back(inputs.astype(jnp.float32), dnormed, 1e-05)).astype(jnp.bfloat16)
            dkey_pre = norm_back(key_pre, dkey_hat, 1e-06).astype(jnp.bfloat16).reshape(VIS, KVH * HD)
            dvalue_cast = dvalue.astype(jnp.bfloat16).reshape(VIS, KVH * HD)
            vision_grad = vision_grad + jnp.dot(dkey_pre, key_weight[layer_at].T, preferred_element_type=jnp.float32) + jnp.dot(dvalue_cast, value_weight[layer_at].T, preferred_element_type=jnp.float32)
            dkey_total = dkey_total.at[layer_at].add(jnp.dot(vis_rows.T, dkey_pre, preferred_element_type=jnp.float32))
            dvalue_total = dvalue_total.at[layer_at].add(jnp.dot(vis_rows.T, dvalue_cast, preferred_element_type=jnp.float32))
            grads_all[layer_at].append(dinputs)
            upstream = dinputs
        vision_all.append(vision_grad)
    hidden_states = jnp.stack([jnp.concatenate(hidden_all[layer_at], axis=0) for layer_at in range(LAYERS)])
    text_grads = jnp.stack([jnp.concatenate(grads_all[layer_at], axis=0) for layer_at in range(LAYERS)])
    return (hidden_states, text_grads, jnp.concatenate(vision_all, axis=0), dkey_total, dvalue_total)
```

```python
import functools
import math

import jax
import jax.numpy as jnp
from jax import lax
from jax.experimental import pallas as pl
from jax.experimental.pallas import tpu as pltpu
from jax.sharding import PartitionSpec as P

HD = 128
QGROUP = 8
SEQ = 128
TBLK = 16
TILES = 4
TILE_ROWS = 64
VIS = 256
CHUNKS = 4


def shifted(value, axis, steps):
    count = lax.axis_size(axis)
    first, last = (max(0, -steps), min(count, count - steps))
    return lax.ppermute(value, axis, [(source, source + steps) for source in range(first, last)])


def normalize(values, epsilon):
    return values * lax.rsqrt(jnp.mean(values * values, axis=-1, keepdims=True) + epsilon)


def norm_back(values, upstream, epsilon):
    inv_rms = lax.rsqrt(jnp.mean(values * values, axis=-1, keepdims=True) + epsilon)
    normed = values * inv_rms
    return inv_rms * (upstream - normed * jnp.mean(upstream * normed, axis=-1, keepdims=True))


def allowed_mask(table, tile_count, text_count):
    tile_ok = jnp.arange(TILES, dtype=jnp.int32) < tile_count
    block_ok = (table > 0) & tile_ok[None, :]
    full_mask = jnp.broadcast_to(
        block_ok[:, None, :, None], (SEQ // TBLK, TBLK, TILES, TILE_ROWS)
    ).reshape(SEQ, VIS)
    row_ok = jnp.arange(SEQ, dtype=jnp.int32) < text_count
    return full_mask & row_ok[:, None]


def token_rows(shard, transform):
    return transform(lax.all_gather(shard, "tensor", axis=0, tiled=True), jnp.int32(0))


def token_sums(term, shard_rows):
    return lax.psum_scatter(
        term(jnp.int32(0), shard_rows * lax.axis_size("tensor")).astype(jnp.bfloat16),
        "tensor",
        scatter_dimension=0,
        tiled=True,
    ).astype(jnp.float32)


def kv_totals(keys_part, values_part):
    return lax.psum((keys_part, values_part), "tensor")


def per_device_general(
    text,
    vision,
    query_weight,
    key_weight,
    value_weight,
    out_weight,
    gate,
    cotangent,
    tile_table,
    vision_tiles,
    text_lengths,
):
    layers = lax.axis_size("depth")
    section_index = lax.axis_index("depth")
    tensor_index = lax.axis_index("tensor")
    w_query = query_weight[0]
    w_key = key_weight[0]
    w_value = value_weight[0]
    w_out = out_weight[0]
    gate_value = jnp.tanh(gate[0])
    local_width = w_query.shape[1]
    local_heads = local_width // HD
    kv_width = w_key.shape[1]
    kv_heads = kv_width // HD
    shard_rows = text.shape[0]
    inv_sqrt = 1.0 / math.sqrt(HD)
    kv_group = tensor_index * local_heads // QGROUP
    allowed = allowed_mask(tile_table[0], vision_tiles[0], text_lengths[0])
    row_live = jnp.any(allowed, axis=-1).astype(jnp.float32)
    vis_full = lax.all_gather(vision, "depth", axis=0, tiled=True)
    keys_part = jnp.dot(vis_full, w_key, preferred_element_type=jnp.float32)
    values_part = jnp.dot(vis_full, w_value, preferred_element_type=jnp.float32)
    keys_pre, values_pre = kv_totals(keys_part, values_part)
    keys_cast = (
        normalize(keys_pre.reshape(VIS, kv_heads, HD), 1e-06)
        .astype(jnp.bfloat16)
        .reshape(VIS, kv_width)
    )
    values_cast = values_pre.astype(jnp.bfloat16)
    key_group = lax.dynamic_slice_in_dim(keys_cast, kv_group * HD, HD, 1)
    value_group = lax.dynamic_slice_in_dim(values_cast, kv_group * HD, HD, 1)
    current = text
    for layer_at in range(layers):

        def project(rows_in, offset):
            normed = normalize(rows_in.astype(jnp.float32), 1e-05).astype(jnp.bfloat16)
            return jnp.dot(normed, w_query, preferred_element_type=jnp.float32)

        layer_queries = token_rows(current, project).reshape(SEQ, local_heads, HD)
        layer_query_cast = normalize(layer_queries, 1e-06).astype(jnp.bfloat16)
        scores = (
            jnp.einsum(
                "shd,vd->hsv", layer_query_cast, key_group, preferred_element_type=jnp.float32
            )
            * inv_sqrt
        )
        expd = jnp.where(allowed[None], jnp.exp(scores), 0.0)
        layer_probs = expd / (
            jnp.sum(expd, axis=-1, keepdims=True) + (1.0 - row_live)[None, :, None]
        )
        layer_probs_cast = layer_probs.astype(jnp.bfloat16)
        mixed = jnp.einsum(
            "hsv,vd->shd", layer_probs_cast, value_group, preferred_element_type=jnp.float32
        )
        mixed_cast = mixed.astype(jnp.bfloat16).reshape(SEQ, local_width)

        def out_term(offset, number):
            return jnp.dot(mixed_cast, w_out, preferred_element_type=jnp.float32)

        attended = token_sums(out_term, shard_rows)
        outputs = (current.astype(jnp.float32) + gate_value * attended).astype(jnp.bfloat16)
        outputs, kept = (outputs, (layer_queries, layer_query_cast, layer_probs, layer_probs_cast))
        chosen = section_index == layer_at
        if layer_at == 0:
            saved_in, saved_out, saved_kept = (current, outputs, kept)
        else:
            saved_in = jnp.where(chosen, current, saved_in)
            saved_out = jnp.where(chosen, outputs, saved_out)
            saved_kept = jax.tree.map(
                lambda fresh, older: jnp.where(chosen, fresh, older), kept, saved_kept
            )
        if layer_at + 1 < layers:
            current = shifted(outputs, "depth", 1)
    upstream = cotangent
    for layer_at in reversed(range(layers)):
        queries, query_cast, probs, probs_cast = saved_kept
        scaled = (gate_value * upstream.astype(jnp.float32)).astype(jnp.bfloat16)

        def back_project(rows_in, offset):
            return jnp.einsum("sd,kd->sk", rows_in, w_out, preferred_element_type=jnp.float32)

        dmixed = token_rows(scaled, back_project).astype(jnp.bfloat16).reshape(SEQ, local_heads, HD)
        dprobs = jnp.einsum("shd,vd->hsv", dmixed, value_group, preferred_element_type=jnp.float32)
        layer_dvalues = jnp.einsum(
            "hsv,shd->vd", probs_cast, dmixed, preferred_element_type=jnp.float32
        )
        dscores = (
            probs * (dprobs - jnp.sum(probs * dprobs, axis=-1, keepdims=True)) * inv_sqrt
        ).astype(jnp.bfloat16)
        dquery_hat = jnp.einsum(
            "hsv,vd->shd", dscores, key_group, preferred_element_type=jnp.float32
        )
        layer_dkeys_hat = jnp.einsum(
            "hsv,shd->vd", dscores, query_cast, preferred_element_type=jnp.float32
        )
        dquery = (
            norm_back(queries, dquery_hat, 1e-06).astype(jnp.bfloat16).reshape(SEQ, local_width)
        )

        def in_term(offset, number):
            return jnp.einsum("sk,dk->sd", dquery, w_query, preferred_element_type=jnp.float32)

        dnormed = token_sums(in_term, shard_rows)
        dinputs = (
            upstream.astype(jnp.float32) + norm_back(saved_in.astype(jnp.float32), dnormed, 1e-05)
        ).astype(jnp.bfloat16)
        dinputs, kv_grads = (dinputs, (layer_dkeys_hat, layer_dvalues))
        chosen = section_index == layer_at
        if layer_at == layers - 1:
            saved_grad, saved_kv = (dinputs, kv_grads)
        else:
            saved_grad = jnp.where(chosen, dinputs, saved_grad)
            saved_kv = jax.tree.map(
                lambda fresh, older: jnp.where(chosen, fresh, older), kv_grads, saved_kv
            )
        if layer_at > 0:
            upstream = shifted(dinputs, "depth", -1)
    dkeys_hat, dvalues = saved_kv
    one_hot = (jnp.arange(kv_heads, dtype=jnp.int32) == kv_group).astype(jnp.float32)
    dkeys_full = (dkeys_hat[:, None, :] * one_hot[None, :, None]).reshape(VIS, kv_width)
    dvalues_full = (dvalues[:, None, :] * one_hot[None, :, None]).reshape(VIS, kv_width)
    dkeys_total, dvalues_total = kv_totals(dkeys_full, dvalues_full)
    dkeys_cast = (
        norm_back(
            keys_pre.reshape(VIS, kv_heads, HD), dkeys_total.reshape(VIS, kv_heads, HD), 1e-06
        )
        .astype(jnp.bfloat16)
        .reshape(VIS, kv_width)
    )
    dvalues_cast = dvalues_total.astype(jnp.bfloat16)
    dvision_part = jnp.einsum(
        "vc,dc->vd", dkeys_cast, w_key, preferred_element_type=jnp.float32
    ) + jnp.einsum("vc,dc->vd", dvalues_cast, w_value, preferred_element_type=jnp.float32)
    dvision = lax.psum_scatter(dvision_part, "depth", scatter_dimension=0, tiled=True)
    dkey_part = jnp.einsum("vd,vc->dc", vis_full, dkeys_cast, preferred_element_type=jnp.float32)
    dvalue_part = jnp.einsum(
        "vd,vc->dc", vis_full, dvalues_cast, preferred_element_type=jnp.float32
    )
    dkey_grad, dvalue_grad = (
        lax.psum_scatter(dkey_part, "dp", scatter_dimension=1, tiled=True),
        lax.psum_scatter(dvalue_part, "dp", scatter_dimension=1, tiled=True),
    )
    return (saved_out[None], saved_grad[None], dvision, dkey_grad[None], dvalue_grad[None])


F32 = jnp.float32
BF16 = jnp.bfloat16
AG_AT = 0
RS_AT = AG_AT + 2 * CHUNKS * 4
HOP_AT = RS_AT + 2 * CHUNKS * 4
KV_AT = HOP_AT + CHUNKS
KVG_AT = KV_AT + 7
DKR_AT = KVG_AT + 3
DKA_AT = DKR_AT + 3
VIS_AT = DKA_AT + 7
VISX_AT = VIS_AT + 1
DKX_AT = VIS_AT + 2
DV_AT = VIS_AT + 3
SEMS = VIS_AT + 4


def dot_nn(a, b):
    return lax.dot_general(a, b, (((1,), (0,)), ((), ())), preferred_element_type=F32)


def dot_nt(a, b):
    return lax.dot_general(a, b, (((1,), (1,)), ((), ())), preferred_element_type=F32)


def dot_tn(a, b):
    return lax.dot_general(a, b, (((0,), (0,)), ((), ())), preferred_element_type=F32)


def layers_kernel(
    text, vision, cot, wq_hbm, wk_hbm, wv_hbm, wo_hbm, gate, table, tile_count, text_count,
    hid_out, grad_out, dvis_out, dkey_out, dvalue_out,
    wq, wk, wv, wo, rows, term, pair, summed, arrived, hop_in, hop_out, acc_ref,
    vis, vis_other, kv_part, kv_arrived, kv_all, key_pre, mask, qs, probs, mixed, dmixed, dq,
    dk_part, dk_arrived, dk_all, dk_other, dvis_send, dvis_arrived, wsem, ssem, rsem,
):
    dp, depth, me = lax.axis_index("dp"), lax.axis_index("depth"), lax.axis_index("tensor")
    z, core = me // 2, lax.rem(me, 2)
    group, member = me // 4, lax.rem(me, 4)
    width = text.shape[1]
    step = width // CHUNKS
    inv_sqrt = 1.0 / math.sqrt(HD)

    def cols(k):
        return pl.ds(k * step, step)

    def remote(source, target, at, **device):
        return pltpu.make_async_remote_copy(
            src_ref=source, dst_ref=target, send_sem=ssem.at[at], recv_sem=rsem.at[at],
            device_id=device, device_id_type=pl.DeviceIdType.MESH,
        )

    def at_z(offset):
        return lax.rem(z + offset, 4) * 2 + core

    def gather_z(slot, k, offset):
        mine = rows.at[slot, core, z, :, cols(k)]
        return remote(mine, mine, AG_AT + (slot * CHUNKS + k) * 4 + offset, tensor=at_z(offset))

    def gather_pair(slot, k):
        half = rows.at[slot, core, :, :, cols(k)]
        return remote(half, half, AG_AT + (slot * CHUNKS + k) * 4, tensor=z * 2 + 1 - core)

    def gather_start(slot, k):
        for offset in (1, 2, 3):
            gather_z(slot, k, offset).start()

    def gather_turn(slot, k):
        for offset in (1, 2, 3):
            gather_z(slot, k, offset).wait_recv()
        gather_pair(slot, k).start()

    def gathered(slot, k):
        gather_pair(slot, k).wait_recv()
        return rows[slot, :, :, :, cols(k)].reshape(SEQ, step)

    def sum_pair(slot, k):
        return remote(
            term.at[slot, 1 - core, :, cols(k)], pair.at[slot, :, cols(k)],
            RS_AT + (slot * CHUNKS + k) * 4, tensor=z * 2 + 1 - core,
        )

    def sum_z(slot, k, offset):
        return remote(
            summed.at[slot, lax.rem(z + offset, 4), :, cols(k)],
            arrived.at[slot, offset - 1, :, cols(k)],
            RS_AT + (slot * CHUNKS + k) * 4 + offset, tensor=at_z(offset),
        )

    def sum_turn(slot, k):
        sum_pair(slot, k).wait_recv()
        total = term[slot, core, :, cols(k)].astype(F32) + pair[slot, :, cols(k)].astype(F32)
        summed[slot, :, :, cols(k)] = total.astype(BF16).reshape(4, TBLK, step)
        for offset in (1, 2, 3):
            sum_z(slot, k, offset).start()

    def sum_terms(slot, make):
        for k in range(CHUNKS):
            value = make(k).astype(BF16)
            term[slot, 0, :, cols(k)] = value[: SEQ // 2]
            term[slot, 1, :, cols(k)] = value[SEQ // 2 :]
            sum_pair(slot, k).start()
            if k > 0:
                sum_turn(slot, k - 1)
        sum_turn(slot, CHUNKS - 1)

    def sum_result(slot, k):
        for offset in (1, 2, 3):
            sum_z(slot, k, offset).wait_recv()
        total = summed[slot, z, :, cols(k)].astype(F32)
        for offset in (1, 2, 3):
            total += arrived[slot, offset - 1, :, cols(k)].astype(F32)
        return total

    def hop(k):
        return remote(hop_out.at[:, cols(k)], hop_in.at[:, cols(k)], HOP_AT + k, depth=1 - depth)

    def vis_copy():
        return remote(vision, vis.at[depth], VIS_AT, depth=1 - depth)

    def vis_other_copy():
        return remote(vis, vis_other, VISX_AT, dp=1 - dp)

    def kv_send(offset):
        other = lax.rem(me + offset, 8)
        return remote(
            kv_part.at[other], kv_arrived.at[offset - 1], KV_AT + offset - 1, tensor=other
        )

    def in_group(offset):
        return group * 4 + lax.rem(member + offset, 4)

    def kv_share(offset):
        return remote(
            kv_all.at[member], kv_all.at[member], KVG_AT + offset - 1, tensor=in_group(offset)
        )

    def dk_send(offset):
        return remote(
            dk_part.at[lax.rem(member + offset, 4)], dk_arrived.at[offset - 1],
            DKR_AT + offset - 1, tensor=in_group(offset),
        )

    def dk_share(offset):
        return remote(
            dk_all.at[me], dk_all.at[me], DKA_AT + offset - 1, tensor=lax.rem(me + offset, 8)
        )

    def dk_other_copy():
        return remote(dk_all.at[pl.ds((1 - dp) * 4, 4)], dk_other, DKX_AT, dp=1 - dp)

    def dvis_copy():
        return remote(dvis_send, dvis_arrived, DV_AT, depth=1 - depth)

    loads = [
        pltpu.make_async_copy(source.at[0], target, wsem.at[at])
        for at, (source, target) in enumerate(
            ((wk_hbm, wk), (wv_hbm, wv), (wq_hbm, wq), (wo_hbm, wo))
        )
    ]
    for load in loads:
        load.start()
    barrier = pltpu.get_barrier_semaphore()
    for offset in range(1, 8):
        pl.semaphore_signal(
            barrier, inc=1, device_id={"tensor": lax.rem(me + offset, 8)},
            device_id_type=pl.DeviceIdType.MESH,
        )
    pl.semaphore_signal(
        barrier, inc=1, device_id={"depth": 1 - depth}, device_id_type=pl.DeviceIdType.MESH
    )
    pl.semaphore_signal(
        barrier, inc=1, device_id={"dp": 1 - dp}, device_id_type=pl.DeviceIdType.MESH
    )
    pl.semaphore_wait(barrier, 9)

    vis_copy().start()
    for k in range(CHUNKS):
        rows[0, core, z, :, cols(k)] = jnp.where(depth == 0, text[:, cols(k)], cot[:, cols(k)])
        gather_start(0, k)
    vis[depth] = vision[...]

    lane_tile = lax.broadcasted_iota(jnp.int32, (TBLK, VIS), 1) // TILE_ROWS
    row_at = lax.broadcasted_iota(jnp.int32, (TBLK, VIS), 0)
    for block in range(SEQ // TBLK):
        table_row = (block % 4) * 2 + block // 4
        allowed = jnp.zeros((TBLK, VIS), F32)
        for tile in range(TILES):
            on = jnp.where((table[0, table_row, tile] > 0) & (tile < tile_count[0]), 1.0, 0.0)
            allowed = jnp.where(lane_tile == tile, on, allowed)
        allowed = jnp.where(row_at + table_row * TBLK < text_count[0], allowed, 0.0)
        mask[pl.ds(block * TBLK, TBLK), :] = allowed
    gate_value = jnp.tanh(jnp.full((TBLK, HD), gate[0], F32))[:, :1]
    gate_rows = jnp.tanh(jnp.full((SEQ, HD), gate[0], F32))[:, :1]

    vis_copy().wait_recv()
    vis_other_copy().start()
    loads[0].wait()
    loads[1].wait()
    states = vis[...].reshape(VIS, vision.shape[1])
    keys = dot_nn(states, wk[...]).astype(BF16)
    values = dot_nn(states, wv[...]).astype(BF16)
    for owner in range(8):
        here, head = pl.ds((owner % 4) * 64, 64), owner // 4
        at = (owner % 4) * 64
        kv_part[owner, :, :HD] = keys[at : at + 64, head * HD : (head + 1) * HD]
        kv_part[owner, :, HD:] = values[at : at + 64, head * HD : (head + 1) * HD]
    for offset in range(1, 8):
        kv_send(offset).start()

    def kv_reduce():
        for offset in range(1, 8):
            kv_send(offset).wait_recv()
        total = kv_part[me].astype(F32)
        for offset in range(1, 8):
            total += kv_arrived[offset - 1].astype(F32)
        pre = total[:, :HD]
        key_pre[...] = pre
        kv_all[member, :, :HD] = normalize(pre, 1e-06).astype(BF16)
        kv_all[member, :, HD:] = total[:, HD:].astype(BF16)
        for offset in (1, 2, 3):
            kv_share(offset).start()

    def project(slot, query, between=None):
        total = jnp.zeros((SEQ, wq.shape[1]), F32)
        squares = jnp.zeros((SEQ, 1), F32)
        for k in range(CHUNKS):
            block = gathered(slot, k)
            if query:
                total += dot_nn(block, wq[cols(k), :])
                wide = block.astype(F32)
                squares += jnp.sum(wide * wide, axis=-1, keepdims=True)
            else:
                total += dot_nt(block, wo[:, cols(k)])
            if between is not None and k == CHUNKS // 2 - 1:
                between()
        if query:
            return total * lax.rsqrt(squares * (1.0 / width) + 1e-05)
        return (total * gate_rows).astype(BF16)

    def heads():
        return kv_all[:, :, :HD].reshape(VIS, HD), kv_all[:, :, HD:].reshape(VIS, HD)

    def attend(query):
        keys_cast, values_cast = heads()
        allowed = mask[...]
        dead = 1.0 - jnp.max(allowed, axis=-1, keepdims=True)
        for head in range(2):
            own = query[:, head * HD : (head + 1) * HD]
            qs[head] = own
            own_cast = normalize(own, 1e-06).astype(BF16)
            expd = jnp.where(allowed > 0, jnp.exp(dot_nt(own_cast, keys_cast) * inv_sqrt), 0.0)
            weights = expd / (jnp.sum(expd, axis=-1, keepdims=True) + dead)
            probs[head] = weights
            mixed[:, head * HD : (head + 1) * HD] = dot_nn(
                weights.astype(BF16), values_cast
            ).astype(BF16)

    def attend_back():
        keys_cast, values_cast = heads()
        dkeys = jnp.zeros((VIS, HD), F32)
        dvalues = jnp.zeros((VIS, HD), F32)
        for head in range(2):
            own, weights = qs[head], probs[head]
            own_cast = normalize(own, 1e-06).astype(BF16)
            upstream = dmixed[:, head * HD : (head + 1) * HD]
            dprobs = dot_nt(upstream, values_cast)
            dvalues += dot_tn(weights.astype(BF16), upstream)
            dscores = (
                weights
                * (dprobs - jnp.sum(weights * dprobs, axis=-1, keepdims=True))
                * inv_sqrt
            ).astype(BF16)
            dkeys += dot_tn(dscores, own_cast)
            dq[:, head * HD : (head + 1) * HD] = norm_back(
                own, dot_nn(dscores, keys_cast), 1e-06
            ).astype(BF16)
        dk_part[:, :, :HD] = dkeys.astype(BF16).reshape(4, 64, HD)
        dk_part[:, :, HD:] = dvalues.astype(BF16).reshape(4, 64, HD)

    def out_term(k):
        return dot_nn(mixed[...], wo[:, cols(k)])

    def in_term(k):
        return dot_nt(dq[...], wq[cols(k), :])

    def token_grad(slot, inputs, upstream):
        squares = jnp.zeros((TBLK, 1), F32)
        along = jnp.zeros((TBLK, 1), F32)
        for k in range(CHUNKS):
            dnormed = sum_result(slot, k)
            acc_ref[:, cols(k)] = dnormed
            wide = inputs[:, cols(k)].astype(F32)
            squares += jnp.sum(wide * wide, axis=-1, keepdims=True)
            along += jnp.sum(wide * dnormed, axis=-1, keepdims=True)
        inv_rms = lax.rsqrt(squares * (1.0 / width) + 1e-05)
        scale = along * (1.0 / width) * inv_rms * inv_rms
        for k in range(CHUNKS):
            wide = inputs[:, cols(k)].astype(F32)
            grad_out[0, :, cols(k)] = (
                upstream[:, cols(k)].astype(F32)
                + inv_rms * (acc_ref[:, cols(k)] - wide * scale)
            ).astype(BF16)

    def layer_output(slot, k, inputs):
        fresh = inputs[:, cols(k)].astype(F32) + gate_value * sum_result(slot, k)
        hid_out[0, :, cols(k)] = fresh.astype(BF16)

    def take_hop():
        for k in range(CHUNKS):
            hop(k).wait_recv()
            rows[1, core, z, :, cols(k)] = hop_in[:, cols(k)]
            gather_start(1, k)
        for k in range(CHUNKS):
            gather_turn(1, k)

    def kv_ready():
        for offset in (1, 2, 3):
            kv_share(offset).wait_recv()

    loads[2].wait()
    loads[3].wait()
    for k in range(CHUNKS):
        gather_turn(0, k)
    kv_reduce()

    @pl.when(depth == 0)
    def _():
        query = project(0, True)
        kv_ready()
        attend(query)
        sum_terms(0, out_term)
        for k in range(CHUNKS):
            layer_output(0, k, text)
            hop_out[:, cols(k)] = hid_out[0, :, cols(k)]
            hop(k).start()
        take_hop()
        dmixed[...] = project(1, False)
        attend_back()
        for offset in (1, 2, 3):
            dk_send(offset).start()
        sum_terms(1, in_term)

    @pl.when(depth == 1)
    def _():
        dmixed[...] = project(0, False)
        kv_ready()
        take_hop()
        attend(project(1, True))
        attend_back()
        sum_terms(0, in_term)
        token_grad(0, hop_in, cot)
        for k in range(CHUNKS):
            hop_out[:, cols(k)] = grad_out[0, :, cols(k)]
            hop(k).start()
        for offset in (1, 2, 3):
            dk_send(offset).start()
        sum_terms(1, out_term)

    for offset in (1, 2, 3):
        dk_send(offset).wait_recv()
    total = dk_part[member].astype(F32)
    for offset in (1, 2, 3):
        total += dk_arrived[offset - 1].astype(F32)
    dk_all[me, :, :HD] = norm_back(key_pre[...], total[:, :HD], 1e-06).astype(BF16)
    dk_all[me, :, HD:] = total[:, HD:].astype(BF16)
    for offset in range(1, 8):
        dk_share(offset).start()
    for offset in range(1, 8):
        dk_share(offset).wait_recv()
    dk_other_copy().start()

    def dvision(half):
        first = dk_all[pl.ds(half * 2, 2)].reshape(VIS // 2, 2 * HD)
        second = dk_all[pl.ds(4 + half * 2, 2)].reshape(VIS // 2, 2 * HD)
        dkeys = jnp.concatenate([first[:, :HD], second[:, :HD]], axis=1)
        dvalues = jnp.concatenate([first[:, HD:], second[:, HD:]], axis=1)
        return dot_nt(dkeys, wk[...]) + dot_nt(dvalues, wv[...])

    dvis_send[...] = dvision(1 - depth).astype(BF16)
    dvis_copy().start()
    dvis_out[...] = dvision(depth)
    vis_other_copy().wait_recv()
    grads = dot_tn(
        vis[...].reshape(VIS, vision.shape[1]), dk_all[pl.ds(dp * 4, 4)].reshape(VIS, 2 * HD)
    )
    dk_other_copy().wait_recv()
    grads += dot_tn(
        vis_other[...].reshape(VIS, vision.shape[1]), dk_other[...].reshape(VIS, 2 * HD)
    )
    dkey_out[0] = grads[:, :HD]
    dvalue_out[0] = grads[:, HD:]

    @pl.when(depth == 0)
    def _():
        token_grad(1, text, hop_in)

    @pl.when(depth == 1)
    def _():
        for k in range(CHUNKS):
            layer_output(1, k, hop_in)

    dvis_copy().wait_recv()
    dvis_out[...] += dvis_arrived[...].astype(F32)

    sent = [vis_copy(), vis_other_copy(), dk_other_copy(), dvis_copy()]
    sent += [kv_send(offset) for offset in range(1, 8)]
    sent += [dk_share(offset) for offset in range(1, 8)]
    for offset in (1, 2, 3):
        sent += [kv_share(offset), dk_send(offset)]
    for k in range(CHUNKS):
        sent.append(hop(k))
        for slot in range(2):
            sent += [gather_pair(slot, k), sum_pair(slot, k)]
            for offset in (1, 2, 3):
                sent += [gather_z(slot, k, offset), sum_z(slot, k, offset)]
    for copy in sent:
        copy.wait_send()


def per_device(
    text, vision, query_weight, key_weight, value_weight, out_weight, gate, cotangent,
    tile_table, vision_tiles, text_lengths,
):
    n_dp, n_depth, n_tensor = (lax.axis_size(name) for name in ("dp", "depth", "tensor"))
    shard, width = text.shape
    features, kv_width = vision.shape[1], key_weight.shape[2]
    local = query_weight.shape[2]
    plain = (n_dp, n_depth, n_tensor, shard, local) == (2, 2, 8, TBLK, 2 * HD)
    if not (plain and kv_width == 2 * HD and width % (CHUNKS * 2 * HD) == 0):
        return per_device_general(
            text, vision, query_weight, key_weight, value_weight, out_weight, gate, cotangent,
            tile_table, vision_tiles, text_lengths,
        )
    vmem = pl.BlockSpec(memory_space=pltpu.VMEM)
    smem = pl.BlockSpec(memory_space=pltpu.SMEM)
    whole = pl.BlockSpec(memory_space=pl.ANY)
    grad_columns = kv_width // n_dp
    return pl.pallas_call(
        layers_kernel,
        out_shape=(
            jax.ShapeDtypeStruct((1, shard, width), BF16),
            jax.ShapeDtypeStruct((1, shard, width), BF16),
            jax.ShapeDtypeStruct((VIS // 2, features), F32),
            jax.ShapeDtypeStruct((1, features, grad_columns), F32),
            jax.ShapeDtypeStruct((1, features, grad_columns), F32),
        ),
        in_specs=[vmem] * 3 + [whole] * 4 + [smem] * 4,
        out_specs=(vmem,) * 5,
        scratch_shapes=[
            pltpu.VMEM((width, local), BF16),
            pltpu.VMEM((features, kv_width), BF16),
            pltpu.VMEM((features, kv_width), BF16),
            pltpu.VMEM((local, width), BF16),
            pltpu.VMEM((2, 2, 4, TBLK, width), BF16),
            pltpu.VMEM((2, 2, SEQ // 2, width), BF16),
            pltpu.VMEM((2, SEQ // 2, width), BF16),
            pltpu.VMEM((2, 4, TBLK, width), BF16),
            pltpu.VMEM((2, 3, TBLK, width), BF16),
            pltpu.VMEM((TBLK, width), BF16),
            pltpu.VMEM((TBLK, width), BF16),
            pltpu.VMEM((TBLK, width), F32),
            pltpu.VMEM((2, VIS // 2, features), BF16),
            pltpu.VMEM((2, VIS // 2, features), BF16),
            pltpu.VMEM((8, 64, 2 * HD), BF16),
            pltpu.VMEM((7, 64, 2 * HD), BF16),
            pltpu.VMEM((4, 64, 2 * HD), BF16),
            pltpu.VMEM((64, HD), F32),
            pltpu.VMEM((SEQ, VIS), F32),
            pltpu.VMEM((2, SEQ, HD), F32),
            pltpu.VMEM((2, SEQ, VIS), F32),
            pltpu.VMEM((SEQ, local), BF16),
            pltpu.VMEM((SEQ, local), BF16),
            pltpu.VMEM((SEQ, local), BF16),
            pltpu.VMEM((4, 64, 2 * HD), BF16),
            pltpu.VMEM((3, 64, 2 * HD), BF16),
            pltpu.VMEM((8, 64, 2 * HD), BF16),
            pltpu.VMEM((4, 64, 2 * HD), BF16),
            pltpu.VMEM((VIS // 2, features), BF16),
            pltpu.VMEM((VIS // 2, features), BF16),
            pltpu.SemaphoreType.DMA((4,)),
            pltpu.SemaphoreType.DMA((SEMS,)),
            pltpu.SemaphoreType.DMA((SEMS,)),
        ],
        compiler_params=pltpu.CompilerParams(
            collective_id=0, has_side_effects=True, vmem_limit_bytes=52 * 1024 * 1024
        ),
        cost_estimate=pl.CostEstimate(
            flops=6_000_000_000, bytes_accessed=16_000_000, transcendentals=100_000
        ),
    )(
        text, vision, cotangent, query_weight, key_weight, value_weight, out_weight, gate,
        tile_table, vision_tiles, text_lengths,
    )


def solution(mesh):
    in_specs = (
        P(("dp", "tensor"), None),
        P(("dp", "depth"), "tensor"),
        P("depth", None, "tensor"),
        P("depth", "tensor", None),
        P("depth", "tensor", None),
        P("depth", "tensor", None),
        P("depth"),
        P(("dp", "tensor"), None),
        P("dp", None, None),
        P("dp"),
        P("dp"),
    )
    out_specs = (
        P("depth", ("dp", "tensor"), None),
        P("depth", ("dp", "tensor"), None),
        P(("dp", "depth"), "tensor"),
        P("depth", "tensor", "dp"),
        P("depth", "tensor", "dp"),
    )
    return jax.shard_map(
        per_device, mesh=mesh, in_specs=in_specs, out_specs=out_specs, check_vma=False
    )
```

```python
import functools
import math

import jax
import jax.numpy as jnp
from jax import lax
from jax.experimental import pallas as pl
from jax.experimental.pallas import tpu as pltpu
from jax.sharding import PartitionSpec as P

HD = 128
QGROUP = 8
SEQ = 128
TBLK = 16
TILES = 4
TILE_ROWS = 64
VIS = 256
CHUNKS = 4


def shifted(value, axis, steps):
    count = lax.axis_size(axis)
    first, last = (max(0, -steps), min(count, count - steps))
    return lax.ppermute(value, axis, [(source, source + steps) for source in range(first, last)])


def normalize(values, epsilon):
    return values * lax.rsqrt(jnp.mean(values * values, axis=-1, keepdims=True) + epsilon)


def norm_back(values, upstream, epsilon):
    inv_rms = lax.rsqrt(jnp.mean(values * values, axis=-1, keepdims=True) + epsilon)
    normed = values * inv_rms
    return inv_rms * (upstream - normed * jnp.mean(upstream * normed, axis=-1, keepdims=True))


def allowed_mask(table, tile_count, text_count):
    tile_ok = jnp.arange(TILES, dtype=jnp.int32) < tile_count
    block_ok = (table > 0) & tile_ok[None, :]
    full_mask = jnp.broadcast_to(
        block_ok[:, None, :, None], (SEQ // TBLK, TBLK, TILES, TILE_ROWS)
    ).reshape(SEQ, VIS)
    row_ok = jnp.arange(SEQ, dtype=jnp.int32) < text_count
    return full_mask & row_ok[:, None]


def token_rows(shard, transform):
    return transform(lax.all_gather(shard, "tensor", axis=0, tiled=True), jnp.int32(0))


def token_sums(term, shard_rows):
    return lax.psum_scatter(
        term(jnp.int32(0), shard_rows * lax.axis_size("tensor")).astype(jnp.bfloat16),
        "tensor",
        scatter_dimension=0,
        tiled=True,
    ).astype(jnp.float32)


def kv_totals(keys_part, values_part):
    return lax.psum((keys_part, values_part), "tensor")


def per_device_general(
    text,
    vision,
    query_weight,
    key_weight,
    value_weight,
    out_weight,
    gate,
    cotangent,
    tile_table,
    vision_tiles,
    text_lengths,
):
    layers = lax.axis_size("depth")
    section_index = lax.axis_index("depth")
    tensor_index = lax.axis_index("tensor")
    w_query = query_weight[0]
    w_key = key_weight[0]
    w_value = value_weight[0]
    w_out = out_weight[0]
    gate_value = jnp.tanh(gate[0])
    local_width = w_query.shape[1]
    local_heads = local_width // HD
    kv_width = w_key.shape[1]
    kv_heads = kv_width // HD
    shard_rows = text.shape[0]
    inv_sqrt = 1.0 / math.sqrt(HD)
    kv_group = tensor_index * local_heads // QGROUP
    allowed = allowed_mask(tile_table[0], vision_tiles[0], text_lengths[0])
    row_live = jnp.any(allowed, axis=-1).astype(jnp.float32)
    vis_full = lax.all_gather(vision, "depth", axis=0, tiled=True)
    keys_part = jnp.dot(vis_full, w_key, preferred_element_type=jnp.float32)
    values_part = jnp.dot(vis_full, w_value, preferred_element_type=jnp.float32)
    keys_pre, values_pre = kv_totals(keys_part, values_part)
    keys_cast = (
        normalize(keys_pre.reshape(VIS, kv_heads, HD), 1e-06)
        .astype(jnp.bfloat16)
        .reshape(VIS, kv_width)
    )
    values_cast = values_pre.astype(jnp.bfloat16)
    key_group = lax.dynamic_slice_in_dim(keys_cast, kv_group * HD, HD, 1)
    value_group = lax.dynamic_slice_in_dim(values_cast, kv_group * HD, HD, 1)
    current = text
    for layer_at in range(layers):

        def project(rows_in, offset):
            normed = normalize(rows_in.astype(jnp.float32), 1e-05).astype(jnp.bfloat16)
            return jnp.dot(normed, w_query, preferred_element_type=jnp.float32)

        layer_queries = token_rows(current, project).reshape(SEQ, local_heads, HD)
        layer_query_cast = normalize(layer_queries, 1e-06).astype(jnp.bfloat16)
        scores = (
            jnp.einsum(
                "shd,vd->hsv", layer_query_cast, key_group, preferred_element_type=jnp.float32
            )
            * inv_sqrt
        )
        expd = jnp.where(allowed[None], jnp.exp(scores), 0.0)
        layer_probs = expd / (
            jnp.sum(expd, axis=-1, keepdims=True) + (1.0 - row_live)[None, :, None]
        )
        layer_probs_cast = layer_probs.astype(jnp.bfloat16)
        mixed = jnp.einsum(
            "hsv,vd->shd", layer_probs_cast, value_group, preferred_element_type=jnp.float32
        )
        mixed_cast = mixed.astype(jnp.bfloat16).reshape(SEQ, local_width)

        def out_term(offset, number):
            return jnp.dot(mixed_cast, w_out, preferred_element_type=jnp.float32)

        attended = token_sums(out_term, shard_rows)
        outputs = (current.astype(jnp.float32) + gate_value * attended).astype(jnp.bfloat16)
        outputs, kept = (outputs, (layer_queries, layer_query_cast, layer_probs, layer_probs_cast))
        chosen = section_index == layer_at
        if layer_at == 0:
            saved_in, saved_out, saved_kept = (current, outputs, kept)
        else:
            saved_in = jnp.where(chosen, current, saved_in)
            saved_out = jnp.where(chosen, outputs, saved_out)
            saved_kept = jax.tree.map(
                lambda fresh, older: jnp.where(chosen, fresh, older), kept, saved_kept
            )
        if layer_at + 1 < layers:
            current = shifted(outputs, "depth", 1)
    upstream = cotangent
    for layer_at in reversed(range(layers)):
        queries, query_cast, probs, probs_cast = saved_kept
        scaled = (gate_value * upstream.astype(jnp.float32)).astype(jnp.bfloat16)

        def back_project(rows_in, offset):
            return jnp.einsum("sd,kd->sk", rows_in, w_out, preferred_element_type=jnp.float32)

        dmixed = token_rows(scaled, back_project).astype(jnp.bfloat16).reshape(SEQ, local_heads, HD)
        dprobs = jnp.einsum("shd,vd->hsv", dmixed, value_group, preferred_element_type=jnp.float32)
        layer_dvalues = jnp.einsum(
            "hsv,shd->vd", probs_cast, dmixed, preferred_element_type=jnp.float32
        )
        dscores = (
            probs * (dprobs - jnp.sum(probs * dprobs, axis=-1, keepdims=True)) * inv_sqrt
        ).astype(jnp.bfloat16)
        dquery_hat = jnp.einsum(
            "hsv,vd->shd", dscores, key_group, preferred_element_type=jnp.float32
        )
        layer_dkeys_hat = jnp.einsum(
            "hsv,shd->vd", dscores, query_cast, preferred_element_type=jnp.float32
        )
        dquery = (
            norm_back(queries, dquery_hat, 1e-06).astype(jnp.bfloat16).reshape(SEQ, local_width)
        )

        def in_term(offset, number):
            return jnp.einsum("sk,dk->sd", dquery, w_query, preferred_element_type=jnp.float32)

        dnormed = token_sums(in_term, shard_rows)
        dinputs = (
            upstream.astype(jnp.float32) + norm_back(saved_in.astype(jnp.float32), dnormed, 1e-05)
        ).astype(jnp.bfloat16)
        dinputs, kv_grads = (dinputs, (layer_dkeys_hat, layer_dvalues))
        chosen = section_index == layer_at
        if layer_at == layers - 1:
            saved_grad, saved_kv = (dinputs, kv_grads)
        else:
            saved_grad = jnp.where(chosen, dinputs, saved_grad)
            saved_kv = jax.tree.map(
                lambda fresh, older: jnp.where(chosen, fresh, older), kv_grads, saved_kv
            )
        if layer_at > 0:
            upstream = shifted(dinputs, "depth", -1)
    dkeys_hat, dvalues = saved_kv
    one_hot = (jnp.arange(kv_heads, dtype=jnp.int32) == kv_group).astype(jnp.float32)
    dkeys_full = (dkeys_hat[:, None, :] * one_hot[None, :, None]).reshape(VIS, kv_width)
    dvalues_full = (dvalues[:, None, :] * one_hot[None, :, None]).reshape(VIS, kv_width)
    dkeys_total, dvalues_total = kv_totals(dkeys_full, dvalues_full)
    dkeys_cast = (
        norm_back(
            keys_pre.reshape(VIS, kv_heads, HD), dkeys_total.reshape(VIS, kv_heads, HD), 1e-06
        )
        .astype(jnp.bfloat16)
        .reshape(VIS, kv_width)
    )
    dvalues_cast = dvalues_total.astype(jnp.bfloat16)
    dvision_part = jnp.einsum(
        "vc,dc->vd", dkeys_cast, w_key, preferred_element_type=jnp.float32
    ) + jnp.einsum("vc,dc->vd", dvalues_cast, w_value, preferred_element_type=jnp.float32)
    dvision = lax.psum_scatter(dvision_part, "depth", scatter_dimension=0, tiled=True)
    dkey_part = jnp.einsum("vd,vc->dc", vis_full, dkeys_cast, preferred_element_type=jnp.float32)
    dvalue_part = jnp.einsum(
        "vd,vc->dc", vis_full, dvalues_cast, preferred_element_type=jnp.float32
    )
    dkey_grad, dvalue_grad = (
        lax.psum_scatter(dkey_part, "dp", scatter_dimension=1, tiled=True),
        lax.psum_scatter(dvalue_part, "dp", scatter_dimension=1, tiled=True),
    )
    return (saved_out[None], saved_grad[None], dvision, dkey_grad[None], dvalue_grad[None])


F32 = jnp.float32
BF16 = jnp.bfloat16
AG_AT = 0
RS_AT = AG_AT + 2 * CHUNKS * 6
HOP_AT = RS_AT + 2 * CHUNKS * 4
KV_AT = HOP_AT + CHUNKS
KVG_AT = KV_AT + 7
DKR_AT = KVG_AT + 3
DKA_AT = DKR_AT + 3
VIS_AT = DKA_AT + 7
VISX_AT = VIS_AT + 1
DKX_AT = VIS_AT + 2
DV_AT = VIS_AT + 3
SEMS = VIS_AT + 4


def dot_nn(a, b):
    return lax.dot_general(a, b, (((1,), (0,)), ((), ())), preferred_element_type=F32)


def dot_nt(a, b):
    return lax.dot_general(a, b, (((1,), (1,)), ((), ())), preferred_element_type=F32)


def dot_tn(a, b):
    return lax.dot_general(a, b, (((0,), (0,)), ((), ())), preferred_element_type=F32)


def layers_kernel(
    text, vision, cot, wq_hbm, wk_hbm, wv_hbm, wo_hbm, gate, table, tile_count, text_count,
    hid_out, grad_out, dvis_out, dkey_out, dvalue_out,
    wq, wk, wv, wo, rows, term, pair, summed, arrived, hop_in, hop_out, acc_ref,
    vis, vis_other, kv_part, kv_arrived, kv_all, key_pre, mask, qs, probs, mixed, dmixed, dq,
    dk_part, dk_arrived, dk_all, dk_other, dvis_send, dvis_arrived, wsem, ssem, rsem,
):
    dp, depth, me = lax.axis_index("dp"), lax.axis_index("depth"), lax.axis_index("tensor")
    z, core = me // 2, lax.rem(me, 2)
    group, member = me // 4, lax.rem(me, 4)
    width = text.shape[1]
    step = width // CHUNKS
    inv_sqrt = 1.0 / math.sqrt(HD)

    def cols(k):
        return pl.ds(k * step, step)

    def remote(source, target, at, **device):
        return pltpu.make_async_remote_copy(
            src_ref=source, dst_ref=target, send_sem=ssem.at[at], recv_sem=rsem.at[at],
            device_id=device, device_id_type=pl.DeviceIdType.MESH,
        )

    def at_z(offset):
        return lax.rem(z + offset, 4) * 2 + core

    def gather_z(slot, k, source, target, send_at):
        block = rows.at[slot, core, source, :, cols(k)]
        base = AG_AT + (slot * CHUNKS + k) * 6
        return pltpu.make_async_remote_copy(
            src_ref=block, dst_ref=block, send_sem=ssem.at[base + send_at],
            recv_sem=rsem.at[base + 1 + source], device_id={"tensor": target * 2 + core},
            device_id_type=pl.DeviceIdType.MESH,
        )

    def gather_up(slot, k, source):
        return gather_z(slot, k, source, lax.rem(z + 1, 4), 1 + source)

    def gather_down(slot, k, source, send_at):
        return gather_z(slot, k, source, lax.rem(z + 3, 4), send_at)

    def gather_pair(slot, k):
        half = rows.at[slot, core, :, :, cols(k)]
        return remote(half, half, AG_AT + (slot * CHUNKS + k) * 6, tensor=z * 2 + 1 - core)

    def gather_start(slot, k):
        @pl.when(z < 3)
        def _():
            gather_up(slot, k, z).start()

        @pl.when(z > 0)
        def _():
            gather_down(slot, k, z, 5).start()

    def gather_pass(slot, k, far):
        @pl.when(z >= far)
        def _():
            gather_up(slot, k, z - far).wait_recv()

            @pl.when(z < 3)
            def _():
                gather_up(slot, k, z - far).start()

        @pl.when(z + far <= 3)
        def _():
            gather_down(slot, k, z + far, 1 + z + far).wait_recv()

            @pl.when(z > 0)
            def _():
                gather_down(slot, k, z + far, 1 + z + far).start()

    def gather_turn(slot, k):
        gather_pass(slot, k, 3)
        gather_pair(slot, k).start()

    def gather_sent(slot, k):
        gather_pair(slot, k).wait_send()

        @pl.when(z < 3)
        def _():
            gather_up(slot, k, z).wait_send()

        @pl.when(z > 0)
        def _():
            gather_down(slot, k, z, 5).wait_send()

        for far in (1, 2, 3):

            @pl.when((z >= far) & (z < 3))
            def _():
                gather_up(slot, k, z - far).wait_send()

            @pl.when((z + far <= 3) & (z > 0))
            def _():
                gather_down(slot, k, z + far, 1 + z + far).wait_send()

    def gathered(slot, k):
        gather_pair(slot, k).wait_recv()
        return rows[slot, :, :, :, cols(k)].reshape(SEQ, step)

    def sum_pair(slot, k):
        return remote(
            term.at[slot, 1 - core, :, cols(k)], pair.at[slot, :, cols(k)],
            RS_AT + (slot * CHUNKS + k) * 4, tensor=z * 2 + 1 - core,
        )

    def sum_z(slot, k, offset):
        return remote(
            summed.at[slot, lax.rem(z + offset, 4), :, cols(k)],
            arrived.at[slot, offset - 1, :, cols(k)],
            RS_AT + (slot * CHUNKS + k) * 4 + offset, tensor=at_z(offset),
        )

    def sum_turn(slot, k):
        sum_pair(slot, k).wait_recv()
        total = term[slot, core, :, cols(k)].astype(F32) + pair[slot, :, cols(k)].astype(F32)
        summed[slot, :, :, cols(k)] = total.astype(BF16).reshape(4, TBLK, step)
        for offset in (1, 2, 3):
            sum_z(slot, k, offset).start()

    def sum_terms(slot, make):
        for k in range(CHUNKS):
            value = make(k).astype(BF16)
            term[slot, 0, :, cols(k)] = value[: SEQ // 2]
            term[slot, 1, :, cols(k)] = value[SEQ // 2 :]
            sum_pair(slot, k).start()
            if k > 0:
                sum_turn(slot, k - 1)
        sum_turn(slot, CHUNKS - 1)

    def sum_result(slot, k):
        for offset in (1, 2, 3):
            sum_z(slot, k, offset).wait_recv()
        total = summed[slot, z, :, cols(k)].astype(F32)
        for offset in (1, 2, 3):
            total += arrived[slot, offset - 1, :, cols(k)].astype(F32)
        return total

    def hop(k):
        return remote(hop_out.at[:, cols(k)], hop_in.at[:, cols(k)], HOP_AT + k, depth=1 - depth)

    def vis_copy():
        return remote(vision, vis.at[depth], VIS_AT, depth=1 - depth)

    def vis_other_copy():
        return remote(vis, vis_other, VISX_AT, dp=1 - dp)

    def kv_send(offset):
        other = lax.rem(me + offset, 8)
        return remote(
            kv_part.at[other], kv_arrived.at[offset - 1], KV_AT + offset - 1, tensor=other
        )

    def in_group(offset):
        return group * 4 + lax.rem(member + offset, 4)

    def kv_share(offset):
        return remote(
            kv_all.at[member], kv_all.at[member], KVG_AT + offset - 1, tensor=in_group(offset)
        )

    def dk_send(offset):
        return remote(
            dk_part.at[lax.rem(member + offset, 4)], dk_arrived.at[offset - 1],
            DKR_AT + offset - 1, tensor=in_group(offset),
        )

    def dk_share(offset):
        return remote(
            dk_all.at[me], dk_all.at[me], DKA_AT + offset - 1, tensor=lax.rem(me + offset, 8)
        )

    def dk_other_copy():
        return remote(dk_all.at[pl.ds((1 - dp) * 4, 4)], dk_other, DKX_AT, dp=1 - dp)

    def dvis_copy():
        return remote(dvis_send, dvis_arrived, DV_AT, depth=1 - depth)

    loads = [
        pltpu.make_async_copy(source.at[0], target, wsem.at[at])
        for at, (source, target) in enumerate(
            ((wk_hbm, wk), (wv_hbm, wv), (wq_hbm, wq), (wo_hbm, wo))
        )
    ]
    for load in loads:
        load.start()
    barrier = pltpu.get_barrier_semaphore()
    for offset in range(1, 8):
        pl.semaphore_signal(
            barrier, inc=1, device_id={"tensor": lax.rem(me + offset, 8)},
            device_id_type=pl.DeviceIdType.MESH,
        )
    pl.semaphore_signal(
        barrier, inc=1, device_id={"depth": 1 - depth}, device_id_type=pl.DeviceIdType.MESH
    )
    pl.semaphore_signal(
        barrier, inc=1, device_id={"dp": 1 - dp}, device_id_type=pl.DeviceIdType.MESH
    )
    pl.semaphore_wait(barrier, 9)

    vis_copy().start()
    for k in range(CHUNKS):
        rows[0, core, z, :, cols(k)] = jnp.where(depth == 0, text[:, cols(k)], cot[:, cols(k)])
        gather_start(0, k)
    vis[depth] = vision[...]

    lane_tile = lax.broadcasted_iota(jnp.int32, (TBLK, VIS), 1) // TILE_ROWS
    row_at = lax.broadcasted_iota(jnp.int32, (TBLK, VIS), 0)
    for block in range(SEQ // TBLK):
        table_row = (block % 4) * 2 + block // 4
        allowed = jnp.zeros((TBLK, VIS), F32)
        for tile in range(TILES):
            on = jnp.where((table[0, table_row, tile] > 0) & (tile < tile_count[0]), 1.0, 0.0)
            allowed = jnp.where(lane_tile == tile, on, allowed)
        allowed = jnp.where(row_at + table_row * TBLK < text_count[0], allowed, 0.0)
        mask[pl.ds(block * TBLK, TBLK), :] = allowed
    gate_value = jnp.tanh(jnp.full((TBLK, HD), gate[0], F32))[:, :1]
    gate_rows = jnp.tanh(jnp.full((SEQ, HD), gate[0], F32))[:, :1]

    vis_copy().wait_recv()
    vis_other_copy().start()
    loads[0].wait()
    loads[1].wait()
    states = vis[...].reshape(VIS, vision.shape[1])
    keys = dot_nn(states, wk[...]).astype(BF16)
    values = dot_nn(states, wv[...]).astype(BF16)
    for owner in range(8):
        here, head = pl.ds((owner % 4) * 64, 64), owner // 4
        at = (owner % 4) * 64
        kv_part[owner, :, :HD] = keys[at : at + 64, head * HD : (head + 1) * HD]
        kv_part[owner, :, HD:] = values[at : at + 64, head * HD : (head + 1) * HD]
    for offset in range(1, 8):
        kv_send(offset).start()

    def kv_reduce():
        for offset in range(1, 8):
            kv_send(offset).wait_recv()
        total = kv_part[me].astype(F32)
        for offset in range(1, 8):
            total += kv_arrived[offset - 1].astype(F32)
        pre = total[:, :HD]
        key_pre[...] = pre
        kv_all[member, :, :HD] = normalize(pre, 1e-06).astype(BF16)
        kv_all[member, :, HD:] = total[:, HD:].astype(BF16)
        for offset in (1, 2, 3):
            kv_share(offset).start()

    def project(slot, query):
        total = jnp.zeros((SEQ, wq.shape[1]), F32)
        squares = jnp.zeros((SEQ, 1), F32)
        gather_turn(slot, 0)
        for k in range(CHUNKS):
            if k + 1 < CHUNKS:
                gather_turn(slot, k + 1)
            block = gathered(slot, k)
            if query:
                total += dot_nn(block, wq[cols(k), :])
                wide = block.astype(F32)
                squares += jnp.sum(wide * wide, axis=-1, keepdims=True)
            else:
                total += dot_nt(block, wo[:, cols(k)])
        if query:
            return total * lax.rsqrt(squares * (1.0 / width) + 1e-05)
        return (total * gate_rows).astype(BF16)

    def heads():
        return kv_all[:, :, :HD].reshape(VIS, HD), kv_all[:, :, HD:].reshape(VIS, HD)

    def attend(query):
        keys_cast, values_cast = heads()
        allowed = mask[...]
        dead = 1.0 - jnp.max(allowed, axis=-1, keepdims=True)
        for head in range(2):
            own = query[:, head * HD : (head + 1) * HD]
            qs[head] = own
            own_cast = normalize(own, 1e-06).astype(BF16)
            expd = jnp.where(allowed > 0, jnp.exp(dot_nt(own_cast, keys_cast) * inv_sqrt), 0.0)
            weights = expd / (jnp.sum(expd, axis=-1, keepdims=True) + dead)
            probs[head] = weights
            mixed[:, head * HD : (head + 1) * HD] = dot_nn(
                weights.astype(BF16), values_cast
            ).astype(BF16)

    def attend_back():
        keys_cast, values_cast = heads()
        dkeys = jnp.zeros((VIS, HD), F32)
        dvalues = jnp.zeros((VIS, HD), F32)
        for head in range(2):
            own, weights = qs[head], probs[head]
            own_cast = normalize(own, 1e-06).astype(BF16)
            upstream = dmixed[:, head * HD : (head + 1) * HD]
            dprobs = dot_nt(upstream, values_cast)
            dvalues += dot_tn(weights.astype(BF16), upstream)
            dscores = (
                weights
                * (dprobs - jnp.sum(weights * dprobs, axis=-1, keepdims=True))
                * inv_sqrt
            ).astype(BF16)
            dkeys += dot_tn(dscores, own_cast)
            dq[:, head * HD : (head + 1) * HD] = norm_back(
                own, dot_nn(dscores, keys_cast), 1e-06
            ).astype(BF16)
        dk_part[:, :, :HD] = dkeys.astype(BF16).reshape(4, 64, HD)
        dk_part[:, :, HD:] = dvalues.astype(BF16).reshape(4, 64, HD)

    def out_term(k):
        return dot_nn(mixed[...], wo[:, cols(k)])

    def in_term(k):
        return dot_nt(dq[...], wq[cols(k), :])

    def token_grad(slot, inputs, upstream):
        squares = jnp.zeros((TBLK, 1), F32)
        along = jnp.zeros((TBLK, 1), F32)
        for k in range(CHUNKS):
            dnormed = sum_result(slot, k)
            acc_ref[:, cols(k)] = dnormed
            wide = inputs[:, cols(k)].astype(F32)
            squares += jnp.sum(wide * wide, axis=-1, keepdims=True)
            along += jnp.sum(wide * dnormed, axis=-1, keepdims=True)
        inv_rms = lax.rsqrt(squares * (1.0 / width) + 1e-05)
        scale = along * (1.0 / width) * inv_rms * inv_rms
        for k in range(CHUNKS):
            wide = inputs[:, cols(k)].astype(F32)
            grad_out[0, :, cols(k)] = (
                upstream[:, cols(k)].astype(F32)
                + inv_rms * (acc_ref[:, cols(k)] - wide * scale)
            ).astype(BF16)

    def layer_output(slot, k, inputs):
        fresh = inputs[:, cols(k)].astype(F32) + gate_value * sum_result(slot, k)
        hid_out[0, :, cols(k)] = fresh.astype(BF16)

    def take_hop():
        for k in range(CHUNKS):
            hop(k).wait_recv()
            rows[1, core, z, :, cols(k)] = hop_in[:, cols(k)]
            gather_start(1, k)
            if k > 0:
                gather_pass(1, k - 1, 1)
        gather_pass(1, CHUNKS - 1, 1)
        for k in range(CHUNKS):
            gather_pass(1, k, 2)

    def kv_ready():
        for offset in (1, 2, 3):
            kv_share(offset).wait_recv()

    loads[2].wait()
    loads[3].wait()
    for far in (1, 2):
        for k in range(CHUNKS):
            gather_pass(0, k, far)
    kv_reduce()

    @pl.when(depth == 0)
    def _():
        query = project(0, True)
        kv_ready()
        attend(query)
        sum_terms(0, out_term)
        for k in range(CHUNKS):
            layer_output(0, k, text)
            hop_out[:, cols(k)] = hid_out[0, :, cols(k)]
            hop(k).start()
        take_hop()
        dmixed[...] = project(1, False)
        attend_back()
        for offset in (1, 2, 3):
            dk_send(offset).start()
        sum_terms(1, in_term)

    @pl.when(depth == 1)
    def _():
        dmixed[...] = project(0, False)
        kv_ready()
        take_hop()
        attend(project(1, True))
        attend_back()
        sum_terms(0, in_term)
        token_grad(0, hop_in, cot)
        for k in range(CHUNKS):
            hop_out[:, cols(k)] = grad_out[0, :, cols(k)]
            hop(k).start()
        for offset in (1, 2, 3):
            dk_send(offset).start()
        sum_terms(1, out_term)

    for offset in (1, 2, 3):
        dk_send(offset).wait_recv()
    total = dk_part[member].astype(F32)
    for offset in (1, 2, 3):
        total += dk_arrived[offset - 1].astype(F32)
    dk_all[me, :, :HD] = norm_back(key_pre[...], total[:, :HD], 1e-06).astype(BF16)
    dk_all[me, :, HD:] = total[:, HD:].astype(BF16)
    for offset in range(1, 8):
        dk_share(offset).start()
    for offset in range(1, 8):
        dk_share(offset).wait_recv()
    dk_other_copy().start()

    def dvision(half):
        first = dk_all[pl.ds(half * 2, 2)].reshape(VIS // 2, 2 * HD)
        second = dk_all[pl.ds(4 + half * 2, 2)].reshape(VIS // 2, 2 * HD)
        dkeys = jnp.concatenate([first[:, :HD], second[:, :HD]], axis=1)
        dvalues = jnp.concatenate([first[:, HD:], second[:, HD:]], axis=1)
        return dot_nt(dkeys, wk[...]) + dot_nt(dvalues, wv[...])

    dvis_send[...] = dvision(1 - depth).astype(BF16)
    dvis_copy().start()
    dvis_out[...] = dvision(depth)
    vis_other_copy().wait_recv()
    grads = dot_tn(
        vis[...].reshape(VIS, vision.shape[1]), dk_all[pl.ds(dp * 4, 4)].reshape(VIS, 2 * HD)
    )
    dk_other_copy().wait_recv()
    grads += dot_tn(
        vis_other[...].reshape(VIS, vision.shape[1]), dk_other[...].reshape(VIS, 2 * HD)
    )
    dkey_out[0] = grads[:, :HD]
    dvalue_out[0] = grads[:, HD:]

    @pl.when(depth == 0)
    def _():
        token_grad(1, text, hop_in)

    @pl.when(depth == 1)
    def _():
        for k in range(CHUNKS):
            layer_output(1, k, hop_in)

    dvis_copy().wait_recv()
    dvis_out[...] += dvis_arrived[...].astype(F32)

    sent = [vis_copy(), vis_other_copy(), dk_other_copy(), dvis_copy()]
    sent += [kv_send(offset) for offset in range(1, 8)]
    sent += [dk_share(offset) for offset in range(1, 8)]
    for offset in (1, 2, 3):
        sent += [kv_share(offset), dk_send(offset)]
    for k in range(CHUNKS):
        sent.append(hop(k))
        for slot in range(2):
            gather_sent(slot, k)
            sent.append(sum_pair(slot, k))
            for offset in (1, 2, 3):
                sent.append(sum_z(slot, k, offset))
    for copy in sent:
        copy.wait_send()


def per_device(
    text, vision, query_weight, key_weight, value_weight, out_weight, gate, cotangent,
    tile_table, vision_tiles, text_lengths,
):
    n_dp, n_depth, n_tensor = (lax.axis_size(name) for name in ("dp", "depth", "tensor"))
    shard, width = text.shape
    features, kv_width = vision.shape[1], key_weight.shape[2]
    local = query_weight.shape[2]
    plain = (n_dp, n_depth, n_tensor, shard, local) == (2, 2, 8, TBLK, 2 * HD)
    if not (plain and kv_width == 2 * HD and width % (CHUNKS * 2 * HD) == 0):
        return per_device_general(
            text, vision, query_weight, key_weight, value_weight, out_weight, gate, cotangent,
            tile_table, vision_tiles, text_lengths,
        )
    vmem = pl.BlockSpec(memory_space=pltpu.VMEM)
    smem = pl.BlockSpec(memory_space=pltpu.SMEM)
    whole = pl.BlockSpec(memory_space=pl.ANY)
    grad_columns = kv_width // n_dp
    return pl.pallas_call(
        layers_kernel,
        out_shape=(
            jax.ShapeDtypeStruct((1, shard, width), BF16),
            jax.ShapeDtypeStruct((1, shard, width), BF16),
            jax.ShapeDtypeStruct((VIS // 2, features), F32),
            jax.ShapeDtypeStruct((1, features, grad_columns), F32),
            jax.ShapeDtypeStruct((1, features, grad_columns), F32),
        ),
        in_specs=[vmem] * 3 + [whole] * 4 + [smem] * 4,
        out_specs=(vmem,) * 5,
        scratch_shapes=[
            pltpu.VMEM((width, local), BF16),
            pltpu.VMEM((features, kv_width), BF16),
            pltpu.VMEM((features, kv_width), BF16),
            pltpu.VMEM((local, width), BF16),
            pltpu.VMEM((2, 2, 4, TBLK, width), BF16),
            pltpu.VMEM((2, 2, SEQ // 2, width), BF16),
            pltpu.VMEM((2, SEQ // 2, width), BF16),
            pltpu.VMEM((2, 4, TBLK, width), BF16),
            pltpu.VMEM((2, 3, TBLK, width), BF16),
            pltpu.VMEM((TBLK, width), BF16),
            pltpu.VMEM((TBLK, width), BF16),
            pltpu.VMEM((TBLK, width), F32),
            pltpu.VMEM((2, VIS // 2, features), BF16),
            pltpu.VMEM((2, VIS // 2, features), BF16),
            pltpu.VMEM((8, 64, 2 * HD), BF16),
            pltpu.VMEM((7, 64, 2 * HD), BF16),
            pltpu.VMEM((4, 64, 2 * HD), BF16),
            pltpu.VMEM((64, HD), F32),
            pltpu.VMEM((SEQ, VIS), F32),
            pltpu.VMEM((2, SEQ, HD), F32),
            pltpu.VMEM((2, SEQ, VIS), F32),
            pltpu.VMEM((SEQ, local), BF16),
            pltpu.VMEM((SEQ, local), BF16),
            pltpu.VMEM((SEQ, local), BF16),
            pltpu.VMEM((4, 64, 2 * HD), BF16),
            pltpu.VMEM((3, 64, 2 * HD), BF16),
            pltpu.VMEM((8, 64, 2 * HD), BF16),
            pltpu.VMEM((4, 64, 2 * HD), BF16),
            pltpu.VMEM((VIS // 2, features), BF16),
            pltpu.VMEM((VIS // 2, features), BF16),
            pltpu.SemaphoreType.DMA((4,)),
            pltpu.SemaphoreType.DMA((SEMS,)),
            pltpu.SemaphoreType.DMA((SEMS,)),
        ],
        compiler_params=pltpu.CompilerParams(
            collective_id=0, has_side_effects=True, vmem_limit_bytes=52 * 1024 * 1024
        ),
        cost_estimate=pl.CostEstimate(
            flops=6_000_000_000, bytes_accessed=16_000_000, transcendentals=100_000
        ),
    )(
        text, vision, cotangent, query_weight, key_weight, value_weight, out_weight, gate,
        tile_table, vision_tiles, text_lengths,
    )


def solution(mesh):
    in_specs = (
        P(("dp", "tensor"), None),
        P(("dp", "depth"), "tensor"),
        P("depth", None, "tensor"),
        P("depth", "tensor", None),
        P("depth", "tensor", None),
        P("depth", "tensor", None),
        P("depth"),
        P(("dp", "tensor"), None),
        P("dp", None, None),
        P("dp"),
        P("dp"),
    )
    out_specs = (
        P("depth", ("dp", "tensor"), None),
        P("depth", ("dp", "tensor"), None),
        P(("dp", "depth"), "tensor"),
        P("depth", "tensor", "dp"),
        P("depth", "tensor", "dp"),
    )
    return jax.shard_map(
        per_device, mesh=mesh, in_specs=in_specs, out_specs=out_specs, check_vma=False
    )
```
